32 devices in a mesh: seq: 4 (over y, x), head: 8 (over z, core).
Axes of the slice: x: 2, y: 2, z: 4, core: 2. Of those that a mesh axis runs over, the one named last changes fastest.
Arguments:
- query_rows: bfloat16 [8192, 64, 128], P('seq', 'head'), may hold values from -112 to 112
- key_rows: bfloat16 [8192, 64, 128], P('seq', 'head'), may hold values from -4 to 4
- value_rows: bfloat16 [8192, 64, 128], P('seq', 'head'), may hold values from -6 to 6
- attn_output: bfloat16 [8192, 64, 128], P('seq', 'head'), may hold values from -6 to 6
- out_grad: bfloat16 [8192, 4, 2048], P(('seq', 'head')), may hold values from -6 to 6
- neighbours: int32 [64, 4], replicated, may hold values from 0 to 63, as said below
- counts: int32 [64], replicated, may hold values from 2 to 128
Outputs:
- grad_query: bfloat16 [8192, 4, 2048], P(('seq', 'head'))
- grad_key: bfloat16 [8192, 4, 2048], P(('seq', 'head'))
- grad_value: bfloat16 [8192, 4, 2048], P(('seq', 'head'))
The draws below stay inside these ranges and needn't reach their ends.
Inputs may be any that keep to these rules, and one draw needn't show every extreme that they name: `neighbours`: row t lists 4 different tiles, the first being t itself, each at most half of 16 tiles away from t.
All inputs are finite; a program needn't handle non-finite values.
Results may differ from the reference program's by a relative error of at most 0.011.
Values may be sent and summed in bfloat16 or wider, within the bound.
A program may use at most 256 MiB of HBM per device.

```python
import jax
import jax.numpy as jnp
from jax import lax

DH = 128
TILE = 128
NBR = 4
B = 4
TILES_DEV = 16
D = 2048
ITEMS = 64
TILES = 64
L = 8192


def paired_draw(key):
    base_key = jax.random.fold_in(key, 11)
    query_key, keys_key = jax.random.split(base_key, 2)
    query_vals = jax.random.truncated_normal(query_key, -3.9, 3.9, (L, ITEMS, DH), jnp.float32)
    key_vals = jax.random.truncated_normal(keys_key, -3.9, 3.9, (L, ITEMS, DH), jnp.float32)
    return (query_vals, key_vals)


def draw_query_rows(key, part):
    return paired_draw(key)[0].astype(jnp.bfloat16)


def draw_key_rows(key, part):
    return paired_draw(key)[1].astype(jnp.bfloat16)


def draw_neighbours(key, part):
    reach = TILES_DEV // 2
    window = 2 * reach + 1
    own_tile = jnp.arange(TILES, dtype=jnp.int32)[:, None]
    offsets = jnp.arange(window, dtype=jnp.int32)[None, :] - reach
    candidate = own_tile + offsets
    ranking = jax.random.randint(key, (TILES, window), 0, 2 ** 20, jnp.int32) * window + jnp.arange(window, dtype=jnp.int32)[None, :]
    excluded = (candidate < 0) | (candidate >= TILES) | (offsets == 0)
    ranking = jnp.where(excluded, 2 ** 30 + jnp.arange(window, dtype=jnp.int32)[None, :], ranking)
    order = jnp.argsort(ranking, axis=1, stable=True)[:, :NBR - 1]
    picked = jnp.take_along_axis(candidate, order, axis=1)
    return jnp.concatenate([own_tile, picked], axis=1).astype(jnp.int32)


def with_ends(values, stream_key, least, largest):
    longest = values.shape.index(max(values.shape))
    spots = []
    for shift in (0, 1):
        where = [jax.random.randint(jax.random.fold_in(stream_key, axis), (), 0, length) for axis, length in enumerate(values.shape)]
        where[longest] = (where[longest] + shift) % values.shape[longest]
        spots.append(tuple(where))
    return values.at[spots[0]].set(least).at[spots[1]].set(largest)


def shard_levels(key, extent, cuts, least, top_value):
    def one(dim, blocks):
        steps = jax.random.uniform(jax.random.fold_in(jax.random.fold_in(key, 6), dim), (blocks,), jnp.float32, least / len(cuts), top_value / len(cuts))
        return jnp.repeat(jnp.exp(steps), extent[dim] // blocks).reshape((-1,) + (1,) * (len(extent) - dim - 1))

    gain = one(*cuts[0])
    for cut in cuts[1:]:
        gain = gain * one(*cut)
    return gain


def centred(own_key, extent, deviation, bound, cuts=(), kind=jnp.bfloat16):
    loudness = shard_levels(own_key, extent, cuts, -0.22, 0.18) if cuts else 1.0
    drawn = jax.random.normal(own_key, extent, jnp.float32) * deviation * loudness
    return jnp.minimum(jnp.maximum(drawn, -bound), bound).astype(kind)


def setup_inputs(seed: int = 0) -> dict:
    seeds = jax.random.split(jax.random.key(seed), 8)
    return {
        "query_rows": draw_query_rows(jax.random.fold_in(seeds[7], 71), 0),
        "key_rows": draw_key_rows(jax.random.fold_in(seeds[7], 71), 0),
        "value_rows": centred(seeds[2], (L, ITEMS, DH), 1.0, 6.0, ((0, 4), (1, 8))),
        "attn_output": centred(seeds[3], (L, ITEMS, DH), 1.0, 6.0, ((0, 4), (1, 8))),
        "out_grad": centred(seeds[4], (L, B, D), 1.0, 6.0, ((0, 32),)),
        "neighbours": draw_neighbours(jax.random.fold_in(seeds[7], 71), 0),
        "counts": with_ends(jax.random.randint(seeds[6], (TILES,), 2, TILE + 1), jax.random.fold_in(seeds[6], 1), 2, TILE).astype(jnp.int32),
    }


def one_item(arrays, neighbours, key_valid, query_valid):
    query_one, key_one, value_one, output_one, grad_one = arrays
    scale_factor = DH ** -0.5
    grad_one = grad_one * query_valid[:, None].astype(grad_one.dtype)
    query_t = query_one.astype(jnp.float32).reshape(TILES, TILE, DH)
    key_t = key_one.astype(jnp.float32).reshape(TILES, TILE, DH)
    value_t = value_one.astype(jnp.float32).reshape(TILES, TILE, DH)
    output_t = output_one.astype(jnp.float32).reshape(TILES, TILE, DH)
    grad_t = grad_one.astype(jnp.float32).reshape(TILES, TILE, DH)
    key_near = key_t[neighbours]
    value_near = value_t[neighbours]
    valid_near = key_valid[neighbours]
    scores = jnp.einsum('tid,tnjd->tinj', query_t, key_near) * scale_factor
    scores = jnp.where(valid_near[:, None], scores, -jnp.inf)
    row_max = jnp.max(scores, axis=(2, 3), keepdims=True)
    log_total = row_max + jnp.log(jnp.sum(jnp.exp(scores - row_max), axis=(2, 3), keepdims=True))
    attn_probs = jnp.exp(scores - log_total)
    delta = jnp.sum(grad_t * output_t, axis=-1)
    dprobs = jnp.einsum('tid,tnjd->tinj', grad_t, value_near)
    dscore = (attn_probs * (dprobs - delta[:, :, None, None]) * scale_factor).astype(jnp.bfloat16).astype(jnp.float32)
    probs_low = attn_probs.astype(jnp.bfloat16).astype(jnp.float32)
    dquery = jnp.einsum('tinj,tnjd->tid', dscore, key_near)
    dkey_terms = jnp.einsum('tinj,tid->tnjd', dscore, query_t)
    dvalue_terms = jnp.einsum('tinj,tid->tnjd', probs_low, grad_t)
    flat_lists = neighbours.reshape(-1)
    dkey = jnp.zeros((TILES, TILE, DH), jnp.float32).at[flat_lists].add(dkey_terms.reshape(TILES * NBR, TILE, DH))
    dvalue = jnp.zeros((TILES, TILE, DH), jnp.float32).at[flat_lists].add(dvalue_terms.reshape(TILES * NBR, TILE, DH))
    return (dquery.reshape(L, DH).astype(jnp.bfloat16), dkey.reshape(L, DH).astype(jnp.bfloat16), dvalue.reshape(L, DH).astype(jnp.bfloat16))


def reference(query_rows, key_rows, value_rows, attn_output, out_grad, neighbours, counts):
    key_valid = jnp.arange(TILE, dtype=jnp.int32)[None, :] < counts[:, None]
    query_valid = key_valid.reshape(L)
    grad_items = out_grad.reshape(L, ITEMS, DH)
    stacked = tuple(jnp.moveaxis(array, 1, 0) for array in (query_rows, key_rows, value_rows, attn_output, grad_items))
    grad_q, grad_k, grad_v = lax.map(lambda arrays: one_item(arrays, neighbours, key_valid, query_valid), stacked)
    grad_query = jnp.moveaxis(grad_q, 0, 1).reshape(L, B, D)
    grad_key = jnp.moveaxis(grad_k, 0, 1).reshape(L, B, D)
    grad_value = jnp.moveaxis(grad_v, 0, 1).reshape(L, B, D)
    return (grad_query, grad_key, grad_value)
```

```python
import functools

import jax
import jax.numpy as jnp
from jax import lax
from jax.experimental import pallas as pl
from jax.experimental.pallas import tpu as pltpu
from jax.sharding import PartitionSpec as P

TILE = 128
CHUNKS = 4
NT = (((1,), (1,)), ((), ()))
TN = (((0,), (0,)), ((), ()))


def tile_load(ref, head, tile, piece):
    if piece >= TILE:
        per = piece // TILE
        rows = pl.ds(pl.multiple_of((tile % per) * TILE, TILE), TILE)
        return ref[tile // per, head, rows, :]
    per = TILE // piece
    return ref[pl.ds(tile * per, per), head, :, :].reshape(TILE, ref.shape[-1])


def tile_store(ref, head, tile, piece, value):
    if piece >= TILE:
        per = piece // TILE
        rows = pl.ds(pl.multiple_of((tile % per) * TILE, TILE), TILE)
        ref[tile // per, head, rows, :] = value
    else:
        per = TILE // piece
        ref[pl.ds(tile * per, per), head, :, :] = value.reshape(per, piece, ref.shape[-1])


def attention_kernel(
    piece, lists, key_counts, query_counts,
    q_ref, o_ref, g_ref, low_ref, own_low_ref, own_high_ref, high_ref,
    dq_ref, mid_ref, flank_low_ref, flank_high_ref,
    k_ext, v_ext, k_acc, v_acc,
):
    heads, tokens, head_dim = q_ref.shape
    half = tokens // 2
    scale = head_dim ** (-0.5)
    nbr = lists.shape[0] // (tokens // TILE)
    for place, ref in enumerate((low_ref, own_low_ref, own_high_ref, high_ref)):
        k_ext[:, place * half : (place + 1) * half, :] = ref[0]
        v_ext[:, place * half : (place + 1) * half, :] = ref[1]
    k_acc[...] = jnp.zeros_like(k_acc)
    v_acc[...] = jnp.zeros_like(v_acc)
    row = lax.broadcasted_iota(jnp.int32, (TILE, TILE), 0)

    def step(tile, carry):
        picks = [lists[tile * nbr + n] for n in range(nbr)]
        spots = [pl.ds(pl.multiple_of(pick * TILE, TILE), TILE) for pick in picks]
        limits = [key_counts[pick] for pick in picks]
        own_rows = pl.ds(pl.multiple_of(tile * TILE, TILE), TILE)
        query_live = row[:, :head_dim] < query_counts[tile]
        for head in range(heads):
            query = q_ref[head, own_rows, :]
            grad_f = jnp.where(query_live, tile_load(g_ref, head, tile, piece).astype(jnp.float32), 0.0)
            grad = grad_f.astype(jnp.bfloat16)
            product = grad_f * o_ref[head, own_rows, :].astype(jnp.float32)
            delta = jnp.sum(product.T, axis=0, keepdims=True)
            keys = jnp.concatenate([k_ext[head, spot, :] for spot in spots], axis=0)
            values = jnp.concatenate([v_ext[head, spot, :] for spot in spots], axis=0)
            scores = lax.dot_general(keys, query, NT, preferred_element_type=jnp.float32) * scale
            scores = jnp.concatenate(
                [
                    jnp.where(row < limits[n], scores[n * TILE : (n + 1) * TILE], -1e30)
                    for n in range(nbr)
                ],
                axis=0,
            )
            top = jnp.max(scores, axis=0, keepdims=True)
            weights = jnp.exp(scores - top)
            probs = weights * (1.0 / jnp.sum(weights, axis=0, keepdims=True))
            dprobs = lax.dot_general(values, grad, NT, preferred_element_type=jnp.float32)
            dscore = (probs * (dprobs - delta) * scale).astype(jnp.bfloat16)
            probs_low = probs.astype(jnp.bfloat16)
            dquery = lax.dot_general(dscore, keys, TN, preferred_element_type=jnp.float32)
            dkey = jnp.dot(dscore, query, preferred_element_type=jnp.float32)
            dvalue = jnp.dot(probs_low, grad, preferred_element_type=jnp.float32)
            tile_store(dq_ref, head, tile, piece, dquery.astype(jnp.bfloat16))
            for n, spot in enumerate(spots):
                k_acc[head, spot, :] += dkey[n * TILE : (n + 1) * TILE]
                v_acc[head, spot, :] += dvalue[n * TILE : (n + 1) * TILE]
        return carry

    lax.fori_loop(0, tokens // TILE, step, 0)
    pieces = half // piece
    for which, acc in enumerate((k_acc, v_acc)):
        for head in range(heads):
            for ref, start, count in (
                (flank_low_ref, 0, pieces),
                (mid_ref, half, 2 * pieces),
                (flank_high_ref, 3 * half, pieces),
            ):
                part = acc[head, start : start + count * piece, :].astype(jnp.bfloat16)
                ref[:, which, head, :, :] = part.reshape(count, piece, head_dim)


def attention(lists, key_counts, query_counts, q, o, g, low, own_low, own_high, high, first):
    heads, tokens, head_dim = q.shape
    groups, here, piece, _ = g.shape
    half_groups = groups // 2
    step = 2 if here % 2 == 0 else 1
    half = tokens // 2
    nbr = lists.shape[0] // (tokens // TILE)
    rows = pl.BlockSpec((step, tokens, head_dim), lambda i, *_: (i + first // step, 0, 0))
    pieces = pl.BlockSpec((groups, step, piece, head_dim), lambda i, *_: (0, i, 0, 0))
    halves = pl.BlockSpec((2, step, half, head_dim), lambda i, *_: (0, i, 0, 0))

    def outs(count):
        return pl.BlockSpec((count, 2, step, piece, head_dim), lambda i, *_: (0, 0, i, 0, 0))

    def made(*shape):
        return jax.ShapeDtypeStruct(shape, jnp.bfloat16)

    pairs = here * (tokens // TILE) * nbr
    return pl.pallas_call(
        functools.partial(attention_kernel, piece),
        out_shape=(
            made(groups, here, piece, head_dim),
            made(groups, 2, here, piece, head_dim),
            made(half_groups, 2, here, piece, head_dim),
            made(half_groups, 2, here, piece, head_dim),
        ),
        grid_spec=pltpu.PrefetchScalarGridSpec(
            num_scalar_prefetch=3,
            grid=(here // step,),
            in_specs=[rows, rows, pieces, halves, halves, halves, halves],
            out_specs=[pieces, outs(groups), outs(half_groups), outs(half_groups)],
            scratch_shapes=[
                pltpu.VMEM((step, 2 * tokens, head_dim), jnp.bfloat16),
                pltpu.VMEM((step, 2 * tokens, head_dim), jnp.bfloat16),
                pltpu.VMEM((step, 2 * tokens, head_dim), jnp.float32),
                pltpu.VMEM((step, 2 * tokens, head_dim), jnp.float32),
            ],
        ),
        compiler_params=pltpu.CompilerParams(vmem_limit_bytes=52 * 2**20),
        cost_estimate=pl.CostEstimate(
            flops=pairs * 10 * TILE * TILE * head_dim * 4,
            bytes_accessed=here * tokens * head_dim * 2 * 12,
            transcendentals=pairs * TILE * TILE,
        ),
    )(lists, key_counts, query_counts, q, o, g, low, own_low, own_high, high)


def after(value, earlier):
    if earlier is None:
        return value
    return lax.optimization_barrier((value, earlier))[0]


def shift(value, up):
    count = lax.axis_size("seq")
    pairs = [(i, i + 1) if up else (i + 1, i) for i in range(count - 1)]
    return lax.ppermute(value, "seq", pairs)


def exchange(value):
    return lax.all_to_all(value, "head", split_axis=0, concat_axis=0, tiled=True)


def per_device(query_rows, key_rows, value_rows, attn_output, out_grad, neighbours, counts):
    seq_rows, batch, width = out_grad.shape
    tokens, heads, head_dim = query_rows.shape
    groups = lax.axis_size("head")
    nbr = neighbours.shape[1]
    tiles = tokens // TILE
    half = tokens // 2
    chunks = min(CHUNKS, heads)
    here = heads // chunks

    first_tile = lax.axis_index("seq") * tiles
    ext_base = first_tile - tiles // 2
    lists = lax.dynamic_slice_in_dim(neighbours, first_tile, tiles, 0) - ext_base
    lists = jnp.clip(lists, 0, 2 * tiles - 1).reshape(-1)
    padded = jnp.pad(counts, (tiles // 2, tiles // 2))
    key_counts = lax.dynamic_slice_in_dim(padded, first_tile, 2 * tiles, 0)
    query_counts = lax.dynamic_slice_in_dim(counts, first_tile, tiles, 0)

    def kv_half(c, start):
        cut = [
            jnp.swapaxes(a[start : start + half, c * here : (c + 1) * here, :], 0, 1)
            for a in (key_rows, value_rows)
        ]
        return jnp.stack(cut)

    q = jnp.swapaxes(query_rows, 0, 1)
    o = jnp.swapaxes(attn_output, 0, 1)
    grads = jnp.swapaxes(out_grad.reshape(seq_rows, groups, heads, head_dim), 0, 1)
    grads = jnp.swapaxes(grads, 1, 2)

    dq_parts, dkv_parts = [], []
    halo = None
    for c in range(chunks):
        own_low, own_high = kv_half(c, 0), kv_half(c, half)
        send_low, send_high = after((own_low, own_high), halo)
        low, high = shift(send_high, True), shift(send_low, False)
        halo = (low, high)
        g = exchange(grads[:, c * here : (c + 1) * here])
        dq, mid, flank_low, flank_high = attention(
            lists, key_counts, query_counts, q, o, g, low, own_low, own_high, high, c * here
        )
        from_low, from_high = shift(flank_high, True), shift(flank_low, False)
        dq_parts.append(exchange(dq))
        returned = jnp.concatenate([from_low, from_high], axis=0).astype(jnp.float32)
        total = (mid.astype(jnp.float32) + returned).astype(jnp.bfloat16)
        dkv_parts.append(exchange(total))

    def finish(parts):
        whole = jnp.stack(parts, axis=1).reshape(groups * heads, seq_rows, head_dim)
        return jnp.swapaxes(whole, 0, 1).reshape(seq_rows, batch, width)

    return (
        finish(dq_parts),
        finish([part[:, 0] for part in dkv_parts]),
        finish([part[:, 1] for part in dkv_parts]),
    )


def solution(mesh):
    rows = P("seq", "head", None)
    pieces = P(("seq", "head"), None, None)
    return jax.shard_map(
        per_device,
        mesh=mesh,
        in_specs=(rows, rows, rows, rows, pieces, P(), P()),
        out_specs=(pieces, pieces, pieces),
        check_vma=False,
    )
```

```python
import functools

import jax
import jax.numpy as jnp
from jax import lax
from jax.experimental import pallas as pl
from jax.experimental.pallas import tpu as pltpu
from jax.sharding import PartitionSpec as P

TILE = 128
CHUNKS = 4
NT = (((1,), (1,)), ((), ()))
TN = (((0,), (0,)), ((), ()))


def tile_load(ref, head, tile, piece):
    if piece >= TILE:
        per = piece // TILE
        rows = pl.ds(pl.multiple_of((tile % per) * TILE, TILE), TILE)
        return ref[tile // per, head, rows, :]
    per = TILE // piece
    return ref[pl.ds(tile * per, per), head, :, :].reshape(TILE, ref.shape[-1])


def tile_store(ref, head, tile, piece, value):
    if piece >= TILE:
        per = piece // TILE
        rows = pl.ds(pl.multiple_of((tile % per) * TILE, TILE), TILE)
        ref[tile // per, head, rows, :] = value
    else:
        per = TILE // piece
        ref[pl.ds(tile * per, per), head, :, :] = value.reshape(per, piece, ref.shape[-1])


def attention_kernel(
    piece, lists, key_counts, query_counts,
    q_ref, o_ref, g_ref, low_ref, own_low_ref, own_high_ref, high_ref,
    dq_ref, mid_ref, flank_low_ref, flank_high_ref,
    k_ext, v_ext, k_acc, v_acc,
):
    heads, tokens, head_dim = q_ref.shape
    half = tokens // 2
    scale = head_dim ** (-0.5)
    nbr = lists.shape[0] // (tokens // TILE)
    for place, ref in enumerate((low_ref, own_low_ref, own_high_ref, high_ref)):
        k_ext[:, place * half : (place + 1) * half, :] = ref[0]
        v_ext[:, place * half : (place + 1) * half, :] = ref[1]
    k_acc[...] = jnp.zeros_like(k_acc)
    v_acc[...] = jnp.zeros_like(v_acc)
    row = lax.broadcasted_iota(jnp.int32, (TILE, TILE), 0)

    def step(tile, carry):
        picks = [lists[tile * nbr + n] for n in range(nbr)]
        spots = [pl.ds(pl.multiple_of(pick * TILE, TILE), TILE) for pick in picks]
        limits = [key_counts[pick] for pick in picks]
        own_rows = pl.ds(pl.multiple_of(tile * TILE, TILE), TILE)
        query_live = row[:, :head_dim] < query_counts[tile]
        for head in range(heads):
            query = q_ref[head, own_rows, :]
            grad_f = jnp.where(query_live, tile_load(g_ref, head, tile, piece).astype(jnp.float32), 0.0)
            grad = grad_f.astype(jnp.bfloat16)
            product = grad_f * o_ref[head, own_rows, :].astype(jnp.float32)
            delta = jnp.sum(product.T, axis=0, keepdims=True)
            keys = jnp.concatenate([k_ext[head, spot, :] for spot in spots], axis=0)
            values = jnp.concatenate([v_ext[head, spot, :] for spot in spots], axis=0)
            scores = lax.dot_general(keys, query, NT, preferred_element_type=jnp.float32) * scale
            scores = jnp.concatenate(
                [
                    jnp.where(row < limits[n], scores[n * TILE : (n + 1) * TILE], -1e30)
                    for n in range(nbr)
                ],
                axis=0,
            )
            top = jnp.max(scores, axis=0, keepdims=True)
            weights = jnp.exp(scores - top)
            probs = weights * (1.0 / jnp.sum(weights, axis=0, keepdims=True))
            dprobs = lax.dot_general(values, grad, NT, preferred_element_type=jnp.float32)
            dscore = (probs * (dprobs - delta) * scale).astype(jnp.bfloat16)
            probs_low = probs.astype(jnp.bfloat16)
            dquery = lax.dot_general(dscore, keys, TN, preferred_element_type=jnp.float32)
            dkey = jnp.dot(dscore, query, preferred_element_type=jnp.float32)
            dvalue = jnp.dot(probs_low, grad, preferred_element_type=jnp.float32)
            tile_store(dq_ref, head, tile, piece, dquery.astype(jnp.bfloat16))
            for n, spot in enumerate(spots):
                k_acc[head, spot, :] += dkey[n * TILE : (n + 1) * TILE]
                v_acc[head, spot, :] += dvalue[n * TILE : (n + 1) * TILE]
        return carry

    lax.fori_loop(0, tokens // TILE, step, 0)
    pieces = half // piece
    for which, acc in enumerate((k_acc, v_acc)):
        for head in range(heads):
            for ref, start, count in (
                (flank_low_ref, 0, pieces),
                (mid_ref, half, 2 * pieces),
                (flank_high_ref, 3 * half, pieces),
            ):
                part = acc[head, start : start + count * piece, :].astype(jnp.bfloat16)
                ref[:, which, head, :, :] = part.reshape(count, piece, head_dim)


def attention(lists, key_counts, query_counts, q, o, g, low, own_low, own_high, high, first):
    heads, tokens, head_dim = q.shape
    groups, _, piece, _ = g.shape
    here = low.shape[1]
    half_groups = groups // 2
    step = 2 if here % 2 == 0 else 1
    half = tokens // 2
    nbr = lists.shape[0] // (tokens // TILE)
    rows = pl.BlockSpec((step, tokens, head_dim), lambda i, *_: (i + first // step, 0, 0))
    pieces = pl.BlockSpec((groups, step, piece, head_dim), lambda i, *_: (0, i, 0, 0))
    g_pieces = pl.BlockSpec(
        (groups, step, piece, head_dim), lambda i, *_: (0, i + first // step, 0, 0)
    )
    halves = pl.BlockSpec((2, step, half, head_dim), lambda i, *_: (0, i, 0, 0))

    def outs(count):
        return pl.BlockSpec((count, 2, step, piece, head_dim), lambda i, *_: (0, 0, i, 0, 0))

    def made(*shape):
        return jax.ShapeDtypeStruct(shape, jnp.bfloat16)

    pairs = here * (tokens // TILE) * nbr
    return pl.pallas_call(
        functools.partial(attention_kernel, piece),
        out_shape=(
            made(groups, here, piece, head_dim),
            made(groups, 2, here, piece, head_dim),
            made(half_groups, 2, here, piece, head_dim),
            made(half_groups, 2, here, piece, head_dim),
        ),
        grid_spec=pltpu.PrefetchScalarGridSpec(
            num_scalar_prefetch=3,
            grid=(here // step,),
            in_specs=[rows, rows, g_pieces, halves, halves, halves, halves],
            out_specs=[pieces, outs(groups), outs(half_groups), outs(half_groups)],
            scratch_shapes=[
                pltpu.VMEM((step, 2 * tokens, head_dim), jnp.bfloat16),
                pltpu.VMEM((step, 2 * tokens, head_dim), jnp.bfloat16),
                pltpu.VMEM((step, 2 * tokens, head_dim), jnp.float32),
                pltpu.VMEM((step, 2 * tokens, head_dim), jnp.float32),
            ],
        ),
        compiler_params=pltpu.CompilerParams(vmem_limit_bytes=52 * 2**20),
        cost_estimate=pl.CostEstimate(
            flops=pairs * 10 * TILE * TILE * head_dim * 4,
            bytes_accessed=here * tokens * head_dim * 2 * 12,
            transcendentals=pairs * TILE * TILE,
        ),
    )(lists, key_counts, query_counts, q, o, g, low, own_low, own_high, high)


def after(value, earlier):
    if earlier is None:
        return value
    return lax.optimization_barrier((value, earlier))[0]


def shift(value, up):
    count = lax.axis_size("seq")
    pairs = [(i, i + 1) if up else (i + 1, i) for i in range(count - 1)]
    return lax.ppermute(value, "seq", pairs)


def exchange(value):
    return lax.all_to_all(value, "head", split_axis=0, concat_axis=0, tiled=True)


def per_device(query_rows, key_rows, value_rows, attn_output, out_grad, neighbours, counts):
    seq_rows, batch, width = out_grad.shape
    tokens, heads, head_dim = query_rows.shape
    groups = lax.axis_size("head")
    nbr = neighbours.shape[1]
    tiles = tokens // TILE
    half = tokens // 2
    chunks = min(CHUNKS, heads)
    here = heads // chunks

    first_tile = lax.axis_index("seq") * tiles
    ext_base = first_tile - tiles // 2
    lists = lax.dynamic_slice_in_dim(neighbours, first_tile, tiles, 0) - ext_base
    lists = jnp.clip(lists, 0, 2 * tiles - 1).reshape(-1)
    padded = jnp.pad(counts, (tiles // 2, tiles // 2))
    key_counts = lax.dynamic_slice_in_dim(padded, first_tile, 2 * tiles, 0)
    query_counts = lax.dynamic_slice_in_dim(counts, first_tile, tiles, 0)

    def kv_half(c, start):
        cut = [
            jnp.swapaxes(a[start : start + half, c * here : (c + 1) * here, :], 0, 1)
            for a in (key_rows, value_rows)
        ]
        return jnp.stack(cut)

    kv = [(kv_half(c, 0), kv_half(c, half)) for c in range(chunks)]

    def over_seq(rising, falling):
        return shift(rising, True), shift(falling, False)

    halos = [over_seq(kv[0][1], kv[0][0])]
    out_grad = after(out_grad, kv[0])
    grads = jnp.swapaxes(out_grad.reshape(seq_rows, groups, heads, head_dim), 0, 1)
    grads = jnp.swapaxes(grads, 1, 2)
    g = exchange(grads)
    query_rows, attn_output = after((query_rows, attn_output), grads)
    q = jnp.swapaxes(query_rows, 0, 1)
    o = jnp.swapaxes(attn_output, 0, 1)
    for c in range(1, chunks):
        own_low, own_high = after(kv[c], halos[-1])
        halos.append(over_seq(own_high, own_low))

    dq_parts, dk_parts, dv_parts = [], [], []
    for c in range(chunks):
        (low, high), (own_low, own_high) = halos[c], kv[c]
        dq, mid, flank_low, flank_high = attention(
            lists, key_counts, query_counts, q, o, g, low, own_low, own_high, high, c * here
        )
        dq_parts.append(exchange(dq))
        returned = jnp.concatenate(over_seq(flank_high, flank_low), axis=0).astype(jnp.float32)
        total = (mid.astype(jnp.float32) + returned).astype(jnp.bfloat16)
        if c + 1 < chunks:
            both = exchange(total)
            dk_parts.append(both[:, 0])
            dv_parts.append(both[:, 1])
        else:
            dk_parts.append(exchange(total[:, 0]))
            dv_parts.append(exchange(after(total[:, 1], dk_parts[-1])))

    def finish(parts):
        whole = jnp.stack(parts, axis=1).reshape(groups * heads, seq_rows, head_dim)
        return jnp.swapaxes(whole, 0, 1).reshape(seq_rows, batch, width)

    return (
        finish(dq_parts),
        finish(dk_parts),
        finish(dv_parts),
    )


def solution(mesh):
    rows = P("seq", "head", None)
    pieces = P(("seq", "head"), None, None)
    return jax.shard_map(
        per_device,
        mesh=mesh,
        in_specs=(rows, rows, rows, rows, pieces, P(), P()),
        out_specs=(pieces, pieces, pieces),
        check_vma=False,
    )
```

```python
import functools

import jax
import jax.numpy as jnp
from jax import lax
from jax.experimental import pallas as pl
from jax.experimental.pallas import tpu as pltpu
from jax.sharding import PartitionSpec as P

TILE = 128
CHUNKS = 4
NT = (((1,), (1,)), ((), ()))
TN = (((0,), (0,)), ((), ()))


def tile_load(ref, head, tile, piece):
    if piece >= TILE:
        per = piece // TILE
        rows = pl.ds(pl.multiple_of((tile % per) * TILE, TILE), TILE)
        return ref[tile // per, head, rows, :]
    per = TILE // piece
    return ref[pl.ds(tile * per, per), head, :, :].reshape(TILE, ref.shape[-1])


def tile_store(ref, head, tile, piece, value):
    if piece >= TILE:
        per = piece // TILE
        rows = pl.ds(pl.multiple_of((tile % per) * TILE, TILE), TILE)
        ref[tile // per, head, rows, :] = value
    else:
        per = TILE // piece
        ref[pl.ds(tile * per, per), head, :, :] = value.reshape(per, piece, ref.shape[-1])


def attention_kernel(
    piece, lists, key_counts, query_counts,
    q_ref, o_ref, g_ref, low_ref, own_low_ref, own_high_ref, high_ref,
    dq_ref, mid_ref, flank_low_ref, flank_high_ref,
    k_ext, v_ext, k_acc, v_acc,
):
    heads, tokens, head_dim = q_ref.shape
    half = tokens // 2
    scale = head_dim ** (-0.5)
    nbr = lists.shape[0] // (tokens // TILE)
    for place, ref in enumerate((low_ref, own_low_ref, own_high_ref, high_ref)):
        k_ext[:, place * half : (place + 1) * half, :] = ref[0]
        v_ext[:, place * half : (place + 1) * half, :] = ref[1]
    k_acc[...] = jnp.zeros_like(k_acc)
    v_acc[...] = jnp.zeros_like(v_acc)
    row = lax.broadcasted_iota(jnp.int32, (TILE, TILE), 0)

    def step(tile, carry):
        picks = [lists[tile * nbr + n] for n in range(nbr)]
        spots = [pl.ds(pl.multiple_of(pick * TILE, TILE), TILE) for pick in picks]
        limits = [key_counts[pick] for pick in picks]
        own_rows = pl.ds(pl.multiple_of(tile * TILE, TILE), TILE)
        query_live = row[:, :head_dim] < query_counts[tile]
        for head in range(heads):
            query = q_ref[head, own_rows, :]
            grad_f = jnp.where(query_live, tile_load(g_ref, head, tile, piece).astype(jnp.float32), 0.0)
            grad = grad_f.astype(jnp.bfloat16)
            product = grad_f * o_ref[head, own_rows, :].astype(jnp.float32)
            delta = jnp.sum(product.T, axis=0, keepdims=True)
            keys = jnp.concatenate([k_ext[head, spot, :] for spot in spots], axis=0)
            values = jnp.concatenate([v_ext[head, spot, :] for spot in spots], axis=0)
            scores = lax.dot_general(keys, query, NT, preferred_element_type=jnp.float32) * scale
            scores = jnp.concatenate(
                [
                    jnp.where(row < limits[n], scores[n * TILE : (n + 1) * TILE], -1e30)
                    for n in range(nbr)
                ],
                axis=0,
            )
            top = jnp.max(scores, axis=0, keepdims=True)
            weights = jnp.exp(scores - top)
            probs = weights * (1.0 / jnp.sum(weights, axis=0, keepdims=True))
            dprobs = lax.dot_general(values, grad, NT, preferred_element_type=jnp.float32)
            dscore = (probs * (dprobs - delta) * scale).astype(jnp.bfloat16)
            probs_low = probs.astype(jnp.bfloat16)
            dquery = lax.dot_general(dscore, keys, TN, preferred_element_type=jnp.float32)
            dkey = jnp.dot(dscore, query, preferred_element_type=jnp.float32)
            dvalue = jnp.dot(probs_low, grad, preferred_element_type=jnp.float32)
            tile_store(dq_ref, head, tile, piece, dquery.astype(jnp.bfloat16))
            for n, spot in enumerate(spots):
                k_acc[head, spot, :] += dkey[n * TILE : (n + 1) * TILE]
                v_acc[head, spot, :] += dvalue[n * TILE : (n + 1) * TILE]
        return carry

    lax.fori_loop(0, tokens // TILE, step, 0)
    pieces = half // piece
    for which, acc in enumerate((k_acc, v_acc)):
        for head in range(heads):
            for ref, start, count in (
                (flank_low_ref, 0, pieces),
                (mid_ref, half, 2 * pieces),
                (flank_high_ref, 3 * half, pieces),
            ):
                part = acc[head, start : start + count * piece, :].astype(jnp.bfloat16)
                ref[:, which, head, :, :] = part.reshape(count, piece, head_dim)


def attention(lists, key_counts, query_counts, q, o, g, low, own_low, own_high, high, first):
    heads, tokens, head_dim = q.shape
    groups, _, piece, _ = g.shape
    here = low.shape[1]
    half_groups = groups // 2
    step = 2 if here % 2 == 0 else 1
    half = tokens // 2
    nbr = lists.shape[0] // (tokens // TILE)
    rows = pl.BlockSpec((step, tokens, head_dim), lambda i, *_: (i + first // step, 0, 0))
    pieces = pl.BlockSpec((groups, step, piece, head_dim), lambda i, *_: (0, i, 0, 0))
    g_pieces = pl.BlockSpec(
        (groups, step, piece, head_dim), lambda i, *_: (0, i + first // step, 0, 0)
    )
    halves = pl.BlockSpec((2, step, half, head_dim), lambda i, *_: (0, i, 0, 0))

    def outs(count):
        return pl.BlockSpec((count, 2, step, piece, head_dim), lambda i, *_: (0, 0, i, 0, 0))

    def made(*shape):
        return jax.ShapeDtypeStruct(shape, jnp.bfloat16)

    pairs = here * (tokens // TILE) * nbr
    return pl.pallas_call(
        functools.partial(attention_kernel, piece),
        out_shape=(
            made(groups, here, piece, head_dim),
            made(groups, 2, here, piece, head_dim),
            made(half_groups, 2, here, piece, head_dim),
            made(half_groups, 2, here, piece, head_dim),
        ),
        grid_spec=pltpu.PrefetchScalarGridSpec(
            num_scalar_prefetch=3,
            grid=(here // step,),
            in_specs=[rows, rows, g_pieces, halves, halves, halves, halves],
            out_specs=[pieces, outs(groups), outs(half_groups), outs(half_groups)],
            scratch_shapes=[
                pltpu.VMEM((step, 2 * tokens, head_dim), jnp.bfloat16),
                pltpu.VMEM((step, 2 * tokens, head_dim), jnp.bfloat16),
                pltpu.VMEM((step, 2 * tokens, head_dim), jnp.float32),
                pltpu.VMEM((step, 2 * tokens, head_dim), jnp.float32),
            ],
        ),
        compiler_params=pltpu.CompilerParams(vmem_limit_bytes=52 * 2**20),
        cost_estimate=pl.CostEstimate(
            flops=pairs * 10 * TILE * TILE * head_dim * 4,
            bytes_accessed=here * tokens * head_dim * 2 * 12,
            transcendentals=pairs * TILE * TILE,
        ),
    )(lists, key_counts, query_counts, q, o, g, low, own_low, own_high, high)


def after(value, earlier):
    if earlier is None:
        return value
    return lax.optimization_barrier((value, earlier))[0]


def shift(value, up):
    count = lax.axis_size("seq")
    pairs = [(i, i + 1) if up else (i + 1, i) for i in range(count - 1)]
    return lax.ppermute(value, "seq", pairs)


def exchange(value):
    return lax.all_to_all(value, "head", split_axis=0, concat_axis=0, tiled=True)


def per_device(query_rows, key_rows, value_rows, attn_output, out_grad, neighbours, counts):
    seq_rows, batch, width = out_grad.shape
    tokens, heads, head_dim = query_rows.shape
    groups = lax.axis_size("head")
    nbr = neighbours.shape[1]
    tiles = tokens // TILE
    half = tokens // 2
    chunks = min(CHUNKS, heads)
    here = heads // chunks

    first_tile = lax.axis_index("seq") * tiles
    ext_base = first_tile - tiles // 2
    lists = lax.dynamic_slice_in_dim(neighbours, first_tile, tiles, 0) - ext_base
    lists = jnp.clip(lists, 0, 2 * tiles - 1).reshape(-1)
    padded = jnp.pad(counts, (tiles // 2, tiles // 2))
    key_counts = lax.dynamic_slice_in_dim(padded, first_tile, 2 * tiles, 0)
    query_counts = lax.dynamic_slice_in_dim(counts, first_tile, tiles, 0)

    def kv_half(c, start):
        cut = [
            jnp.swapaxes(a[start : start + half, c * here : (c + 1) * here, :], 0, 1)
            for a in (key_rows, value_rows)
        ]
        return jnp.stack(cut)

    kv = [(kv_half(c, 0), kv_half(c, half)) for c in range(chunks)]

    def over_seq(rising, falling):
        return shift(rising, True), shift(falling, False)

    halos = [over_seq(kv[0][1], kv[0][0])]
    out_grad = after(out_grad, kv[0])
    grads = jnp.swapaxes(out_grad.reshape(seq_rows, groups, heads, head_dim), 0, 1)
    grads = jnp.swapaxes(grads, 1, 2)
    g = exchange(grads)
    query_rows, attn_output = after((query_rows, attn_output), grads)
    q = jnp.swapaxes(query_rows, 0, 1)
    o = jnp.swapaxes(attn_output, 0, 1)
    for c in range(1, chunks):
        own_low, own_high = after(kv[c], halos[-1])
        halos.append(over_seq(own_high, own_low))

    def finish(parts):
        whole = jnp.stack(parts, axis=1).reshape(groups * heads, seq_rows, head_dim)
        return jnp.swapaxes(whole, 0, 1).reshape(seq_rows, batch, width)

    dq_parts, dk_parts, dv_parts, made = [], [], [], []
    for c in range(chunks):
        (low, high), (own_low, own_high) = halos[c], kv[c]
        dq, *rest = attention(
            lists, key_counts, query_counts, q, o, g, low, own_low, own_high, high, c * here
        )
        dq_parts.append(exchange(dq))
        made.append(rest)
    grad_query = finish(dq_parts)
    earlier, total = halos[-1], None
    for c, (mid, flank_low, flank_high) in enumerate(made):
        last = c + 1 == chunks
        if last:
            earlier = (earlier, grad_query, total) if c else grad_query
        earlier = over_seq(*after((flank_high, flank_low), earlier))
        returned = jnp.concatenate(earlier, axis=0).astype(jnp.float32)
        total = (mid.astype(jnp.float32) + returned).astype(jnp.bfloat16)
        if last:
            total = after(total, dk_parts[-1] if c else None)
            dk_parts.append(exchange(total[:, 0]))
            grad_key = finish(dk_parts)
            dv_parts.append(exchange(after(total[:, 1], dk_parts[-1])))
        else:
            both = exchange(total)
            dk_parts.append(both[:, 0])
            dv_parts.append(both[:, 1])
    return grad_query, grad_key, finish(dv_parts)


def solution(mesh):
    rows = P("seq", "head", None)
    pieces = P(("seq", "head"), None, None)
    return jax.shard_map(
        per_device,
        mesh=mesh,
        in_specs=(rows, rows, rows, rows, pieces, P(), P()),
        out_specs=(pieces, pieces, pieces),
        check_vma=False,
    )
```
